32 devices in a mesh: groups: 2 (over x), img: 16 (over z, y, core).
Axes of the slice: x: 2, y: 2, z: 4, core: 2. Of those that a mesh axis runs over, the one named last changes fastest.
Arguments:
- features: bfloat16 [256, 64, 1024], P(('groups', 'img')), parts along dimension 0
- partners: int32 [256, 6], P('groups'), parts along dimension 0, may hold values from 0 to 127, as said below
- w_embed: bfloat16 [1024, 768], replicated, may hold values from -0.1875 to 0.1875
- b_embed: float32 [768], replicated, may hold values from -3 to 3
- gain_query: float32 [768], replicated, may hold values from 0.25 to 1.75
- gain_memory: float32 [768], replicated, may hold values from 0.25 to 1.75
- w_query: bfloat16 [768, 768], replicated
- w_key: bfloat16 [768, 768], replicated
- w_value: bfloat16 [768, 768], replicated, may hold values from -0.21875 to 0.21875
- w_out: bfloat16 [768, 768], replicated, may hold values from -0.21875 to 0.21875
- gain_head: float32 [768], replicated, may hold values from 0.25 to 1.75
- w_head: bfloat16 [7, 768], replicated, may hold values from -0.21875 to 0.21875
- b_head: float32 [7], replicated, may hold values from -3 to 3
- points: float32 [256, 3, 64], P(('groups', 'img')), parts along dimension 0, may hold values from -6 to 6
- pair_pose: float32 [12, 1536], P(None, ('groups', 'img')), parts along dimension 1, may hold values from -3 to 3
Outputs:
- new_points: float32 [256, 3, 64], P(('groups', 'img')), parts along dimension 0
- new_pose: float32 [12, 1536], P(None, ('groups', 'img')), parts along dimension 1
- loss: float32 [2], P('groups'), parts along dimension 0
The draws below stay inside these ranges and needn't reach their ends.
There are 2 independent parts, one for each index of `groups`. The reference program is written for one: setup_inputs(seed, part) draws one part's arguments, and reference() takes and returns one part's arrays. A program takes and returns all parts, laid end to end along the dimension named above; an argument that names none is the same for every part. Nothing has to cross between parts.
Inputs may be any that keep to these rules, and one draw needn't show every extreme that they name: `partners`: no pair joins two images of one device. For a device s of img and any other device d, at most 4 pairs have their query image on s and their partner on d; for every s some d receives exactly 4. Images of a device are 8 consecutive numbers.
All inputs are finite; a program needn't handle non-finite values.
Results may differ from the reference program's by a relative error of at most 0.014.
Values may be sent and summed in bfloat16 or wider, within the bound.
A program may use at most 128 MiB of HBM per device.

```python
import jax
import jax.numpy as jnp
from jax import lax

E = 1024
D = 768
HEADS = 12
HEAD_DIM = 64
TOK = 64
IMG_DEV = 8
PAIR_IMG = 6
CAP = 4
IMAGES = 128
PAIRS = 768


def draw_w_query(key, part):
    key = jax.random.fold_in(key, 11)
    own = jax.random.normal(key, (D, D), jnp.float32)
    result = own / D ** 0.5
    return result.astype(jnp.bfloat16)


def draw_w_key(key, part):
    key = jax.random.fold_in(key, 13)
    own = jax.random.normal(key, (D, D), jnp.float32)
    result = own / D ** 0.5
    return result.astype(jnp.bfloat16)


def draw_features(key, part):
    key = jax.random.fold_in(key, 17)
    key_main = jax.random.fold_in(key, 0)
    result = jnp.clip(jax.random.normal(key_main, (IMAGES, TOK, E), jnp.float32), -6.0, 6.0)
    return result.astype(jnp.bfloat16)


def draw_partners(key, part):
    key = jax.random.fold_in(key, 5)
    owners_n = IMAGES // IMG_DEV
    views = IMG_DEV * PAIR_IMG
    span = CAP * (owners_n - 1)

    def block(sub_key, row):
        key_order, key_local = jax.random.split(sub_key)
        order = jax.random.permutation(key_order, span)
        translation_vector = order % (owners_n - 1)
        first = translation_vector[0]
        position = jnp.arange(span)
        score = jnp.where(translation_vector == first, position - span, position)
        chosen = translation_vector[jnp.argsort(score, stable=True)[:views]]
        owner = (row + 1 + chosen) % owners_n
        local = jax.random.randint(key_local, (views,), 0, IMG_DEV)
        return owner * IMG_DEV + local
    result = jax.vmap(block)(jax.random.split(key, owners_n), jnp.arange(owners_n))
    return result.reshape(IMAGES, PAIR_IMG).astype(jnp.int32)


def level_of(own_key, extent, cuts, least, high):
    level = 1.0
    for dim, blocks in cuts:
        heights = jax.random.uniform(jax.random.fold_in(jax.random.fold_in(own_key, 6), dim), (blocks,), jnp.float32, least / len(cuts), high / len(cuts))
        level = level * jnp.repeat(jnp.exp(heights), extent[dim] // blocks).reshape((-1,) + (1,) * (len(extent) - 1 - dim))
    return level


def scatter_about(own_key, extent, scale, reach, shards=(), held_as=jnp.bfloat16):
    drawn = jax.random.normal(own_key, extent, jnp.float32) * scale
    if len(shards) > 0:
        drawn = level_of(own_key, extent, shards, -0.22, 0.18) * drawn
    return jnp.clip(drawn, min=-reach, max=reach).astype(held_as)


def setup_inputs(seed: int = 0, part: int = 0) -> dict:
    arg_keys = jax.random.split(jax.random.key(seed), 16)
    part_keys = jax.random.split(jax.random.fold_in(arg_keys[15], part), 16)
    features = draw_features(jax.random.fold_in(jax.random.fold_in(arg_keys[15], part), 71), part)
    partners = draw_partners(jax.random.fold_in(jax.random.fold_in(arg_keys[15], part), 71), part)
    w_embed = scatter_about(arg_keys[2], (E, D), E ** -0.5, 0.1875)
    b_embed = scatter_about(arg_keys[3], (D,), 0.5, 3.0, (), jnp.float32)
    gain_query = jnp.clip(1.0 + 0.15 * jax.random.normal(arg_keys[4], (D,), jnp.float32), 0.25, 1.75)
    gain_memory = jnp.clip(1.0 + 0.15 * jax.random.normal(arg_keys[5], (D,), jnp.float32), 0.25, 1.75)
    w_query = draw_w_query(jax.random.fold_in(arg_keys[15], 71), part)
    w_key = draw_w_key(jax.random.fold_in(arg_keys[15], 71), part)
    w_value = scatter_about(arg_keys[8], (D, D), D ** -0.5, 0.21875)
    w_out = scatter_about(arg_keys[9], (D, D), D ** -0.5, 0.21875)
    gain_head = jnp.clip(1.0 + 0.15 * jax.random.normal(arg_keys[10], (D,), jnp.float32), 0.25, 1.75)
    w_head = scatter_about(arg_keys[11], (7, D), D ** -0.5, 0.21875)
    b_head = scatter_about(arg_keys[12], (7,), 0.5, 3.0, (), jnp.float32)
    points = scatter_about(part_keys[13], (IMAGES, 3, TOK), 1.0, 6.0, ((0, 16),), jnp.float32)
    pair_pose = scatter_about(part_keys[14], (12, PAIRS), 0.5, 3.0, ((1, 16),), jnp.float32)
    return dict(features=features, partners=partners, w_embed=w_embed, b_embed=b_embed, gain_query=gain_query, gain_memory=gain_memory, w_query=w_query, w_key=w_key, w_value=w_value, w_out=w_out, gain_head=gain_head, w_head=w_head, b_head=b_head, points=points, pair_pose=pair_pose)


def layer_norm(values, gain):
    center = values - lax.optimization_barrier(jnp.mean(values, axis=-1, keepdims=True))
    spread = lax.optimization_barrier(jnp.mean(center * center, axis=-1, keepdims=True))
    return center * lax.rsqrt(spread + 1e-06) * gain

def reference(features, partners, w_embed, b_embed, gain_query, gain_memory, w_query, w_key, w_value, w_out, gain_head, w_head, b_head, points, pair_pose):
    hi = lax.Precision.HIGHEST
    embedded = (jnp.dot(features.reshape(-1, E), w_embed, preferred_element_type=jnp.float32) + b_embed).astype(jnp.bfloat16)
    embed_f = embedded.astype(jnp.float32)
    query_norm = layer_norm(embed_f, gain_query).astype(jnp.bfloat16)
    memory_norm = layer_norm(embed_f, gain_memory).astype(jnp.bfloat16)
    queries = jnp.dot(query_norm, w_query, preferred_element_type=jnp.float32).astype(jnp.bfloat16).reshape(IMAGES, TOK, HEADS, HEAD_DIM)
    keys = jnp.dot(memory_norm, w_key, preferred_element_type=jnp.float32).astype(jnp.bfloat16).reshape(IMAGES, TOK, HEADS, HEAD_DIM)
    values = jnp.dot(memory_norm, w_value, preferred_element_type=jnp.float32).astype(jnp.bfloat16).reshape(IMAGES, TOK, HEADS, HEAD_DIM)
    embed_img = embed_f.reshape(IMAGES, TOK, D)
    pose_cols = pair_pose.T.reshape(IMAGES, PAIR_IMG, 12)
    scale = 1.0 / HEAD_DIM ** 0.5

    def one_image(items):
        query_img, embed_one, partner_row, chi, pose_img = items
        key_rows = jnp.take(keys, partner_row, axis=0).astype(jnp.float32)
        value_rows = jnp.take(values, partner_row, axis=0).astype(jnp.float32)
        scores = jnp.einsum('thd,pshd->phts', query_img.astype(jnp.float32), key_rows) * scale
        top = lax.optimization_barrier(jnp.max(scores, axis=-1, keepdims=True))
        expo = jnp.exp(scores - top)
        weights = (expo / lax.optimization_barrier(jnp.sum(expo, axis=-1, keepdims=True))).astype(jnp.bfloat16)
        attended = jnp.einsum('phts,pshd->pthd', weights.astype(jnp.float32), value_rows).astype(jnp.bfloat16)
        projected = jnp.dot(attended.reshape(-1, D), w_out, preferred_element_type=jnp.float32).reshape(PAIR_IMG, TOK, D)
        decoded = embed_one[None] + projected
        head_in = layer_norm(decoded, gain_head).astype(jnp.bfloat16)
        pred = jnp.einsum('ptd,cd->pct', head_in.astype(jnp.float32), w_head.astype(jnp.float32)) + b_head[None, :, None]
        second_view_point = pred[:, 0:3]
        first_view_point = pred[:, 3:6]
        certainty_level = 1.0 + jnp.exp(pred[:, 6])
        linear_transform = pose_img[:, 0:9].reshape(PAIR_IMG, 3, 3)
        translation_vector = pose_img[:, 9:12]
        second_world_point = jnp.einsum('pab,pbt->pat', linear_transform, second_view_point, precision=hi) + translation_vector[:, :, None]
        first_world_point = jnp.einsum('pab,pbt->pat', linear_transform, first_view_point, precision=hi) + translation_vector[:, :, None]
        second_residual = chi[None] - second_world_point
        grad_q = lax.optimization_barrier(jnp.sum(certainty_level[:, None] * second_residual, axis=0))
        total_q = lax.optimization_barrier(jnp.sum(certainty_level, axis=0))
        gradient_transform = -2.0 * jnp.einsum('pt,pat,pbt->pab', certainty_level, second_residual, second_view_point, precision=hi)
        grad_off = -2.0 * lax.optimization_barrier(jnp.sum(certainty_level[:, None] * second_residual, axis=2))
        denom = 4.0 * lax.optimization_barrier(jnp.sum(certainty_level, axis=1))
        grads = jnp.concatenate([gradient_transform.reshape(PAIR_IMG, 9), grad_off], axis=1)
        pose_next = pose_img - grads / denom[:, None]
        err_q = jnp.sum(certainty_level * lax.optimization_barrier(jnp.sum(second_residual * second_residual, axis=1)))
        return (grad_q, total_q, pose_next, first_world_point, certainty_level, err_q, jnp.sum(certainty_level))
    grad_q, total_q, pose_next, first_world_point, certainty_level, err_q, conf_sum = lax.map(one_image, (queries, embed_img, partners, points, pose_cols))
    chi_p = jnp.take(points, partners.reshape(-1), axis=0).reshape(IMAGES, PAIR_IMG, 3, TOK)
    res_p = chi_p - first_world_point
    flat_ids = partners.reshape(-1)
    grad_p = jax.ops.segment_sum((certainty_level[:, :, None] * res_p).reshape(-1, 3, TOK), flat_ids, num_segments=IMAGES)
    total_p = jax.ops.segment_sum(certainty_level.reshape(-1, TOK), flat_ids, num_segments=IMAGES)
    err_p = jnp.sum(certainty_level * lax.optimization_barrier(jnp.sum(res_p * res_p, axis=2)))
    grad = grad_q + grad_p
    total = total_q + total_p
    new_points = points - 0.5 * grad / total[:, None, :]
    new_pose = pose_next.reshape(PAIRS, 12).T
    loss = ((jnp.sum(err_q) + err_p) / (2.0 * jnp.sum(conf_sum))).reshape(1)
    return (new_points, new_pose, loss)
```

```python
import functools

import jax
import jax.numpy as jnp
from jax import lax
from jax.experimental import pallas as pl
from jax.experimental.pallas import tpu as pltpu
from jax.sharding import PartitionSpec as P

HEADS = 12
IMGS = 8
PER = 6
TOK = 64
VIEWS = IMGS * PER
E = 1024
D = 768
NDEV = 16
ALL = NDEV * IMGS
CHUNKS = 2
CROWS = IMGS * TOK // CHUNKS
CIMG = IMGS // CHUNKS
UP, DOWN, ACROSS, SIB = 0, 1, 2, 3
F32, BF16 = jnp.float32, jnp.bfloat16
HI = lax.Precision.HIGHEST


def norm_rows(values, gain):
    center = values - jnp.mean(values, axis=-1, keepdims=True)
    spread = jnp.mean(center * center, axis=-1, keepdims=True)
    return center * lax.rsqrt(spread + 1e-06) * gain


def dot(a, b, dims=((1,), (0,)), precision=None):
    return lax.dot_general(a, b, (dims, ((), ())), precision=precision, preferred_element_type=F32)


def kernel(
    features,
    partners_s,
    partners_v,
    w_embed,
    b_embed,
    gain_query,
    gain_memory,
    w_query,
    w_key,
    w_value,
    w_out,
    gain_head,
    w_head,
    b_head,
    points,
    pair_pose,
    new_points,
    new_pose,
    loss,
    feat,
    we,
    wq,
    wk,
    wv,
    wo,
    memory,
    keys,
    values,
    embedded,
    query_norm,
    query_diag,
    attended,
    pred,
    all_points,
    outgoing,
    incoming,
    load_sem,
    send_sem,
    recv_sem,
    pts_send,
    pts_recv,
    out_send,
    out_recv,
):
    own = lax.axis_index("img")
    core = own % 2
    y = (own // 2) % 2
    z = own // 4

    barrier = pltpu.get_barrier_semaphore()
    for k in range(1, NDEV):
        pl.semaphore_signal(
            barrier,
            inc=1,
            device_id={"img": (own + k) % NDEV},
            device_id_type=pl.DeviceIdType.MESH,
        )

    loads = []
    for slot, (src, dst) in enumerate(
        [(features, feat), (w_embed, we), (w_query, wq), (w_key, wk), (w_value, wv), (w_out, wo)]
    ):
        copy = pltpu.make_async_copy(src, dst, load_sem.at[slot])
        copy.start()
        loads.append(copy)

    def rank_of(zz, yy, cc):
        return (zz * 2 + yy) * 2 + cc

    targets = {
        UP: own + 4,
        DOWN: own - 4,
        ACROSS: rank_of(z, 1 - y, core),
        SIB: rank_of(z, y, 1 - core),
    }

    def move(piece, way):
        return pltpu.make_async_remote_copy(
            src_ref=memory.at[piece],
            dst_ref=memory.at[piece],
            send_sem=send_sem.at[piece * 4 + way],
            recv_sem=recv_sem.at[piece],
            device_id={"img": targets[way]},
            device_id_type=pl.DeviceIdType.MESH,
        )

    def arrive(piece):
        move(piece, SIB).wait_recv()

    side = z // 2
    near = z * (1 - side) + (3 - z) * side

    def origin_z(j):
        first = (4 - j) // 3 - (3 - j) // 3
        f = (j - near * first) * (1 - side) + (3 - j + near * first) * side
        zero = (3 - j) // 3
        return zero * z + (1 - zero) * f

    def forward_z(oz, piece):
        @pl.when((oz < z) & (z < 3))
        def _():
            move(piece, UP).start()

        @pl.when((oz > z) & (z > 0))
        def _():
            move(piece, DOWN).start()

    def points_copy(peer, slot):
        return pltpu.make_async_remote_copy(
            src_ref=all_points.at[own],
            dst_ref=all_points.at[own],
            send_sem=pts_send.at[slot],
            recv_sem=pts_recv.at[own],
            device_id={"img": peer},
            device_id_type=pl.DeviceIdType.MESH,
        )

    def points_arrive(peer, slot):
        pltpu.make_async_remote_copy(
            src_ref=all_points.at[peer],
            dst_ref=all_points.at[peer],
            send_sem=pts_send.at[slot],
            recv_sem=pts_recv.at[peer],
            device_id={"img": peer},
            device_id_type=pl.DeviceIdType.MESH,
        ).wait_recv()

    all_points[own] = jnp.concatenate(
        [points[:, 0, :], points[:, 1, :], points[:, 2, :], points[:, 2, :]], axis=1
    )

    loads[0].wait()
    loads[1].wait()
    for ch in range(CHUNKS):
        rows = pl.ds(ch * CROWS, CROWS)
        emb = (dot(feat[rows, :], we[...]) + b_embed[...]).astype(BF16)
        embedded[rows, :] = emb
        emb_f = emb.astype(F32)
        center = emb_f - jnp.mean(emb_f, axis=-1, keepdims=True)
        unit = center * lax.rsqrt(jnp.mean(center * center, axis=-1, keepdims=True) + 1e-06)
        memory[own * CHUNKS + ch] = (unit * gain_memory[...]).astype(BF16)
        query_norm[rows, :] = (unit * gain_query[...]).astype(BF16)
        if ch == 0:
            pl.semaphore_wait(barrier, NDEV - 1)
            for k in range(1, NDEV):
                points_copy((own + k) % NDEV, k).start()
        piece = own * CHUNKS + ch

        move(piece, ACROSS).start()

        @pl.when(z < 3)
        def _():
            move(piece, UP).start()

        @pl.when(z > 0)
        def _():
            move(piece, DOWN).start()

        move(piece, SIB).start()

    loads[2].wait()
    group = lax.broadcasted_iota(jnp.int32, (256, 256), 0) // 64
    same_head = group == lax.broadcasted_iota(jnp.int32, (256, 256), 1) // 64

    def make_queries(i, carry):
        rows = pl.ds(pl.multiple_of(i * TOK, TOK), TOK)
        q = dot(query_norm[rows, :], wq[...]).astype(BF16).astype(F32) * 0.125
        for g in range(3):
            part = q[:, g * 256 : (g + 1) * 256]
            stacked = jnp.concatenate([part] * 4, axis=0)
            query_diag[i * 3 + g] = jnp.where(same_head, stacked, 0.0).astype(BF16)
        return carry

    lax.fori_loop(0, IMGS, make_queries, 0)

    loads[3].wait()
    loads[4].wait()
    loads[5].wait()

    def project(piece):
        rows = memory[piece]
        at = pl.ds(piece * CIMG, CIMG)
        keys[at] = dot(rows, wk[...]).astype(BF16).reshape(CIMG, TOK, D)
        values[at] = dot(rows, wv[...]).astype(BF16).reshape(CIMG, TOK, D)

    def exchange(step, carry):
        j = 1 + step // CHUNKS
        ch = step % CHUNKS
        oz = origin_z(j)
        oy = origin_z(j - 1)
        from_z = rank_of(oz, y, core) * CHUNKS + ch
        from_y = rank_of(oy, 1 - y, core) * CHUNKS + ch
        arrive(from_z)
        forward_z(oz, from_z)
        move(from_z, ACROSS).start()
        move(from_z, SIB).start()
        project(from_z)
        arrive(from_y)
        move(from_y, SIB).start()
        project(from_y)
        sib_z = rank_of(oy, y, 1 - core) * CHUNKS + ch
        arrive(sib_z)
        project(sib_z)
        return carry

    lax.fori_loop(0, 3 * CHUNKS, exchange, 0)

    def finish(ch, carry):
        oz = origin_z(3)
        from_y = rank_of(oz, 1 - y, core) * CHUNKS + ch
        arrive(from_y)
        move(from_y, SIB).start()
        sib_z = rank_of(oz, y, 1 - core) * CHUNKS + ch
        arrive(sib_z)
        project(sib_z)
        project(from_y)
        return carry

    def sibling_rest(step, carry):
        sib_y = rank_of(origin_z(step // CHUNKS), 1 - y, 1 - core) * CHUNKS + step % CHUNKS
        arrive(sib_y)
        project(sib_y)
        return carry

    lax.fori_loop(0, 3 * CHUNKS, sibling_rest, 0)
    lax.fori_loop(0, CHUNKS, finish, 0)
    lax.fori_loop(3 * CHUNKS, 4 * CHUNKS, sibling_rest, 0)

    for k in range(1, NDEV):
        points_arrive((own + k) % NDEV, k)
        points_copy((own + k) % NDEV, k).wait_send()

    lane = lax.broadcasted_iota(jnp.int32, (TOK, 128), 1)

    def image(i, carry):
        ids = [partners_s[own * VIEWS + i * PER + p] for p in range(PER)]
        key_rows = jnp.concatenate([keys[ids[p]] for p in range(PER)], axis=0)
        for g in range(3):
            scores = dot(
                key_rows[:, g * 256 : (g + 1) * 256], query_diag[i * 3 + g], ((1,), (1,))
            ).reshape(PER, TOK, 256)
            expo = jnp.exp(scores - jnp.max(scores, axis=1, keepdims=True))
            weights = (expo * (1.0 / jnp.sum(expo, axis=1, keepdims=True))).astype(BF16)
            for p in range(PER):
                for half in range(2):
                    lo = g * 256 + half * 128
                    both = dot(
                        weights[p, :, half * 128 : half * 128 + 128],
                        values[ids[p], :, lo : lo + 128],
                        ((0,), (0,)),
                    )
                    attended[p * TOK : (p + 1) * TOK, lo : lo + 128] = jnp.where(
                        lane < 64, both[:64], both[64:]
                    ).astype(BF16)
        projected = dot(attended[...], wo[...])
        emb_f = embedded[pl.ds(pl.multiple_of(i * TOK, TOK), TOK), :].astype(F32)
        decoded = projected.reshape(PER, TOK, D) + emb_f[None]
        head_in = norm_rows(decoded, gain_head[...].reshape(1, 1, D)).astype(BF16)
        out = dot(w_head[...], head_in.reshape(PER * TOK, D), ((1,), (1,)))
        for p in range(PER):
            pred[p * IMGS + i, 0:7, :] = out[:, p * TOK : (p + 1) * TOK]
        return carry

    lax.fori_loop(0, IMGS, image, 0)

    x = [pred[:, c, :] + b_head[c] for c in range(7)]
    conf = 1.0 + jnp.exp(x[6])
    mine = partners_v[pl.ds(pl.multiple_of(own * IMGS, IMGS), IMGS), :]
    ids = jnp.concatenate([mine[:, p : p + 1] for p in range(PER)], axis=0)
    hot = (ids == lax.broadcasted_iota(jnp.int32, (VIEWS, ALL), 1)).astype(F32)
    row = lax.broadcasted_iota(jnp.int32, (VIEWS, VIEWS), 0)
    col = lax.broadcasted_iota(jnp.int32, (VIEWS, VIEWS), 1)
    perm = ((row % IMGS) * PER + row // IMGS == col).astype(F32)
    pose = dot(perm, pair_pose[...], ((1,), (1,)), HI)
    partner_pts = dot(hot, all_points[...].reshape(ALL, 256), precision=HI)
    res_q, res_p = [], []
    for a in range(3):
        m = [pose[:, 3 * a + b : 3 * a + b + 1] for b in range(3)]
        off = pose[:, 9 + a : 10 + a]
        world_q = m[0] * x[0] + m[1] * x[1] + m[2] * x[2] + off
        world_p = m[0] * x[3] + m[1] * x[4] + m[2] * x[5] + off
        chi = jnp.concatenate([points[:, a, :]] * PER, axis=0)
        res_q.append(chi - world_q)
        res_p.append(partner_pts[:, a * TOK : (a + 1) * TOK] - world_p)
    cq = [conf * r for r in res_q]
    grad_rows = [
        jnp.sum(cq[a] * x[b], axis=1, keepdims=True) for a in range(3) for b in range(3)
    ] + [jnp.sum(cq[a], axis=1, keepdims=True) for a in range(3)]
    conf_row = jnp.sum(conf, axis=1, keepdims=True)
    step = jnp.concatenate(grad_rows, axis=1) * (2.0 / (4.0 * conf_row))
    new_pose[...] = pair_pose[...] + dot(step, perm, ((0,), (0,)), HI)
    err = jnp.sum(
        conf
        * (
            res_q[0] * res_q[0]
            + res_q[1] * res_q[1]
            + res_q[2] * res_q[2]
            + res_p[0] * res_p[0]
            + res_p[1] * res_p[1]
            + res_p[2] * res_p[2]
        )
    )
    conf_sum = 2.0 * jnp.sum(conf_row)
    payload = jnp.concatenate([conf * res_p[0], conf * res_p[1], conf * res_p[2], conf], axis=1)
    sums = dot(hot, payload, ((0,), (0,)), HI)
    outgoing[:, :, 0:256] = sums.reshape(NDEV, IMGS, 256)
    tail_lane = lax.broadcasted_iota(jnp.int32, (NDEV, IMGS, 128), 2)
    outgoing[:, :, 256:384] = jnp.where(tail_lane < 64, err, conf_sum)

    def out_copy(peer, slot):
        return pltpu.make_async_remote_copy(
            src_ref=outgoing.at[peer],
            dst_ref=incoming.at[own],
            send_sem=out_send.at[slot],
            recv_sem=out_recv.at[own],
            device_id={"img": peer},
            device_id_type=pl.DeviceIdType.MESH,
        )

    for k in range(1, NDEV):
        out_copy((own + k) % NDEV, k).start()
    incoming[own] = outgoing[own]

    def fold(values):
        total = values[0:IMGS]
        for p in range(1, PER):
            total = total + values[p * IMGS : (p + 1) * IMGS]
        return total

    total_q = fold(conf)
    grad_q = [fold(c) for c in cq]

    def drain(t, carry):
        j = t // CHUNKS
        ch = t % CHUNKS
        oz = origin_z(j)
        from_z = rank_of(oz, y, core) * CHUNKS + ch
        move(from_z, ACROSS).wait_send()
        move(from_z, SIB).wait_send()
        move(rank_of(oz, 1 - y, core) * CHUNKS + ch, SIB).wait_send()

        @pl.when((oz <= z) & (z < 3))
        def _():
            move(from_z, UP).wait_send()

        @pl.when((oz >= z) & (z > 0))
        def _():
            move(from_z, DOWN).wait_send()

        return carry

    lax.fori_loop(0, 4 * CHUNKS, drain, 0)

    for k in range(1, NDEV):
        peer = (own + k) % NDEV
        pltpu.make_async_remote_copy(
            src_ref=outgoing.at[peer],
            dst_ref=incoming.at[peer],
            send_sem=out_send.at[k],
            recv_sem=out_recv.at[peer],
            device_id={"img": peer},
            device_id_type=pl.DeviceIdType.MESH,
        ).wait_recv()
        out_copy(peer, k).wait_send()
    received = jnp.sum(incoming[...], axis=0)
    total = total_q + received[:, 192:256]
    for a in range(3):
        grad = grad_q[a] + received[:, a * TOK : (a + 1) * TOK]
        new_points[:, a, :] = points[:, a, :] - 0.5 * grad / total
    loss[...] = received[0:1, 256:257] / received[0:1, 320:321]


def fused(*args):
    (
        features,
        partners,
        w_embed,
        b_embed,
        gain_query,
        gain_memory,
        w_query,
        w_key,
        w_value,
        w_out,
        gain_head,
        w_head,
        b_head,
        points,
        pair_pose,
    ) = args
    hbm = pl.BlockSpec(memory_space=pl.ANY)
    vmem = pl.BlockSpec(memory_space=pltpu.VMEM)
    smem = pl.BlockSpec(memory_space=pltpu.SMEM)
    rows = IMGS * TOK
    new_points, new_pose, loss = pl.pallas_call(
        kernel,
        out_shape=(
            jax.ShapeDtypeStruct((IMGS, 3, TOK), F32),
            jax.ShapeDtypeStruct((12, VIEWS), F32),
            jax.ShapeDtypeStruct((1, 1), F32),
        ),
        in_specs=[
            hbm,
            smem,
            vmem,
            hbm,
            vmem,
            vmem,
            vmem,
            hbm,
            hbm,
            hbm,
            hbm,
            vmem,
            vmem,
            smem,
            vmem,
            vmem,
        ],
        out_specs=(vmem, vmem, vmem),
        scratch_shapes=[
            pltpu.VMEM((rows, E), BF16),
            pltpu.VMEM((E, D), BF16),
            pltpu.VMEM((D, D), BF16),
            pltpu.VMEM((D, D), BF16),
            pltpu.VMEM((D, D), BF16),
            pltpu.VMEM((D, D), BF16),
            pltpu.VMEM((NDEV * CHUNKS, CROWS, D), BF16),
            pltpu.VMEM((ALL, TOK, D), BF16),
            pltpu.VMEM((ALL, TOK, D), BF16),
            pltpu.VMEM((rows, D), BF16),
            pltpu.VMEM((rows, D), BF16),
            pltpu.VMEM((IMGS * 3, 256, 256), BF16),
            pltpu.VMEM((PER * TOK, D), BF16),
            pltpu.VMEM((VIEWS, 8, TOK), F32),
            pltpu.VMEM((NDEV, IMGS, 256), F32),
            pltpu.VMEM((NDEV, IMGS, 384), F32),
            pltpu.VMEM((NDEV, IMGS, 384), F32),
            pltpu.SemaphoreType.DMA((6,)),
            pltpu.SemaphoreType.DMA((NDEV * CHUNKS * 4,)),
            pltpu.SemaphoreType.DMA((NDEV * CHUNKS,)),
            pltpu.SemaphoreType.DMA((NDEV,)),
            pltpu.SemaphoreType.DMA((NDEV,)),
            pltpu.SemaphoreType.DMA((NDEV,)),
            pltpu.SemaphoreType.DMA((NDEV,)),
        ],
        compiler_params=pltpu.CompilerParams(
            collective_id=0, has_side_effects=True, vmem_limit_bytes=62 * 1024 * 1024
        ),
    )(
        features.reshape(rows, E),
        partners.reshape(-1),
        partners,
        w_embed,
        b_embed.reshape(1, D),
        gain_query.reshape(1, D),
        gain_memory.reshape(1, D),
        w_query,
        w_key,
        w_value,
        w_out,
        gain_head.reshape(1, D),
        w_head,
        b_head,
        points,
        pair_pose,
    )
    return new_points, new_pose, loss.reshape(1)


def layer_norm(values, gain):
    center = values - jnp.mean(values, axis=-1, keepdims=True)
    spread = jnp.mean(center * center, axis=-1, keepdims=True)
    return center * lax.rsqrt(spread + 1e-06) * gain


def per_device(
    features,
    partners,
    w_embed,
    b_embed,
    gain_query,
    gain_memory,
    w_query,
    w_key,
    w_value,
    w_out,
    gain_head,
    w_head,
    b_head,
    points,
    pair_pose,
):
    maximum_value = lax.Precision.HIGHEST
    count = lax.axis_size("img")
    own_index = lax.axis_index("img")
    img_dev, tokens_img, enc_width = features.shape
    width = w_query.shape[0]
    per_img = partners.shape[1]
    views = img_dev * per_img
    heads = HEADS
    head_size = width // heads
    capacity = max(2, (views + count - 2) // (count - 1))
    slots = count * capacity
    embedded = (
        jnp.dot(features.reshape(-1, enc_width), w_embed, preferred_element_type=jnp.float32)
        + b_embed
    ).astype(jnp.bfloat16)
    embed_f = embedded.astype(jnp.float32)
    query_norm = layer_norm(embed_f, gain_query).astype(jnp.bfloat16)
    memory_norm = layer_norm(embed_f, gain_memory).astype(jnp.bfloat16)
    queries = (
        jnp.dot(query_norm, w_query, preferred_element_type=jnp.float32)
        .astype(jnp.bfloat16)
        .reshape(img_dev, tokens_img, heads, head_size)
    )
    owners = (partners // img_dev).reshape(count, views)
    local_idx = (partners % img_dev).reshape(count, views)
    view_range = jnp.arange(views)
    earlier = view_range[:, None] > view_range[None, :]
    same_owner = owners[:, :, None] == owners[:, None, :]
    rank = jnp.sum(jnp.logical_and(same_owner, earlier[None]), axis=2)
    mine = owners == own_index
    select = jnp.logical_and(
        mine[:, :, None], rank[:, :, None] == jnp.arange(capacity)[None, None, :]
    ).astype(jnp.float32)
    local_hot = (local_idx[:, :, None] == jnp.arange(img_dev)[None, None, :]).astype(jnp.float32)
    pick = jnp.einsum("svc,svl->scl", select, local_hot, precision=maximum_value)
    pick_flat = pick.reshape(slots, img_dev).astype(jnp.bfloat16)
    my_owner = lax.dynamic_index_in_dim(owners, own_index, 0, keepdims=False)
    my_rank = lax.dynamic_index_in_dim(rank, own_index, 0, keepdims=False)
    slot_of_view = my_owner * capacity + my_rank
    placed = jnp.dot(
        pick_flat,
        memory_norm.reshape(img_dev, tokens_img * width),
        preferred_element_type=jnp.float32,
    )
    arrived = lax.all_to_all(
        placed.astype(jnp.bfloat16).reshape(count, capacity, tokens_img, width),
        "img",
        split_axis=0,
        concat_axis=0,
        tiled=True,
    )
    memory_views = jnp.take(
        arrived.reshape(slots, tokens_img, width), slot_of_view, axis=0
    ).reshape(views * tokens_img, width)
    key_views = jnp.dot(memory_views, w_key, preferred_element_type=jnp.float32).astype(
        jnp.bfloat16
    )
    value_views = jnp.dot(memory_views, w_value, preferred_element_type=jnp.float32).astype(
        jnp.bfloat16
    )
    key_views = key_views.reshape(img_dev, per_img, tokens_img, heads, head_size)
    value_views = value_views.reshape(img_dev, per_img, tokens_img, heads, head_size)
    scale = 1.0 / head_size**0.5
    scores = (
        jnp.einsum("ithd,ipshd->iphts", queries, key_views, preferred_element_type=jnp.float32)
        * scale
    )
    top = jnp.max(scores, axis=-1, keepdims=True)
    expo = jnp.exp(scores - top)
    weights = (expo / jnp.sum(expo, axis=-1, keepdims=True)).astype(jnp.bfloat16)
    attended = jnp.einsum(
        "iphts,ipshd->ipthd", weights, value_views, preferred_element_type=jnp.float32
    ).astype(jnp.bfloat16)
    projected = jnp.dot(
        attended.reshape(views * tokens_img, width), w_out, preferred_element_type=jnp.float32
    )
    decoded = embed_f.reshape(img_dev, 1, tokens_img, width) + projected.reshape(
        img_dev, per_img, tokens_img, width
    )
    head_in = layer_norm(decoded, gain_head).astype(jnp.bfloat16)
    pred = (
        jnp.einsum("iptd,cd->ipct", head_in, w_head, preferred_element_type=jnp.float32)
        + b_head[None, None, :, None]
    )
    pred = pred.reshape(views, 7, tokens_img)
    second_view_point = pred[:, 0:3]
    first_view_point = pred[:, 3:6]
    certainty_level = 1.0 + jnp.exp(pred[:, 6])
    pose_rows = pair_pose.T
    linear_transform = pose_rows[:, 0:9].reshape(views, 3, 3)
    translation_vector = pose_rows[:, 9:12]
    second_world_point = (
        jnp.einsum("xdp,xpk->xdk", linear_transform, second_view_point, precision=maximum_value)
        + translation_vector[:, :, None]
    )
    first_world_point = (
        jnp.einsum("xdp,xpk->xdk", linear_transform, first_view_point, precision=maximum_value)
        + translation_vector[:, :, None]
    )
    chi_views = jnp.broadcast_to(points[:, None], (img_dev, per_img, 3, tokens_img)).reshape(
        views, 3, tokens_img
    )
    second_residual = chi_views - second_world_point
    weighted_q = (certainty_level[:, None] * second_residual).reshape(
        img_dev, per_img, 3, tokens_img
    )
    grad_q = jnp.sum(weighted_q, axis=1)
    total_q = jnp.sum(certainty_level.reshape(img_dev, per_img, tokens_img), axis=1)
    gradient_transform = -2.0 * jnp.einsum(
        "zo,zpo,zso->zps",
        certainty_level,
        second_residual,
        second_view_point,
        precision=maximum_value,
    )
    grad_off = -2.0 * jnp.sum(certainty_level[:, None] * second_residual, axis=2)
    denom = 4.0 * jnp.sum(certainty_level, axis=1)
    grads = jnp.concatenate([gradient_transform.reshape(views, 9), grad_off], axis=1)
    new_pose = (pose_rows - grads / denom[:, None]).T
    err_q = jnp.sum(certainty_level * jnp.sum(second_residual * second_residual, axis=1))
    payload = jnp.concatenate([first_world_point, certainty_level[:, None]], axis=1)
    slot_hot = (slot_of_view[:, None] == jnp.arange(slots)[None, :]).astype(jnp.float32)
    outgoing = jnp.einsum("vk,vct->kct", slot_hot, payload, precision=maximum_value).reshape(
        count, capacity, 4, tokens_img
    )
    returned = lax.all_to_all(
        outgoing.astype(jnp.bfloat16), "img", split_axis=0, concat_axis=0, tiled=True
    ).astype(outgoing.dtype)
    ret_world = returned[:, :, 0:3]
    ret_conf = returned[:, :, 3]
    chi_slot = jnp.einsum("scl,lat->scat", pick, points, precision=maximum_value)
    res_p = chi_slot - ret_world
    grad_p = jnp.einsum(
        "scl,scat->lat", pick, ret_conf[:, :, None] * res_p, precision=maximum_value
    )
    total_p = jnp.einsum("scl,sct->lt", pick, ret_conf, precision=maximum_value)
    err_p = jnp.sum(ret_conf * jnp.sum(res_p * res_p, axis=2))
    new_points = points - 0.5 * (grad_q + grad_p) / (total_q + total_p)[:, None, :]
    err_sum, weight_sum = lax.psum((err_q + err_p, 2.0 * jnp.sum(certainty_level)), "img")
    loss = (err_sum / weight_sum).reshape(1)
    return (new_points, new_pose, loss)


def solution(mesh):
    return jax.shard_map(
        fused if mesh.shape["img"] == NDEV else per_device,
        mesh=mesh,
        in_specs=(
            P(("groups", "img"), None, None),
            P("groups", None),
            P(),
            P(),
            P(),
            P(),
            P(),
            P(),
            P(),
            P(),
            P(),
            P(),
            P(),
            P(("groups", "img"), None, None),
            P(None, ("groups", "img")),
        ),
        out_specs=(P(("groups", "img"), None, None), P(None, ("groups", "img")), P("groups")),
        check_vma=False,
    )
```

```python
import functools

import jax
import jax.numpy as jnp
from jax import lax
from jax.experimental import pallas as pl
from jax.experimental.pallas import tpu as pltpu
from jax.sharding import PartitionSpec as P

HEADS = 12
IMGS = 8
PER = 6
TOK = 64
VIEWS = IMGS * PER
E = 1024
D = 768
NDEV = 16
ALL = NDEV * IMGS
CHUNKS = 2
CROWS = IMGS * TOK // CHUNKS
CIMG = IMGS // CHUNKS
UP, DOWN, ACROSS, SIB = 0, 1, 2, 3
F32, BF16 = jnp.float32, jnp.bfloat16
HI = lax.Precision.HIGHEST


def norm_rows(values, gain):
    center = values - jnp.mean(values, axis=-1, keepdims=True)
    spread = jnp.mean(center * center, axis=-1, keepdims=True)
    return center * lax.rsqrt(spread + 1e-06) * gain


def dot(a, b, dims=((1,), (0,)), precision=None):
    return lax.dot_general(a, b, (dims, ((), ())), precision=precision, preferred_element_type=F32)


def kernel(
    features,
    partners,
    w_embed,
    b_embed,
    gain_query,
    gain_memory,
    w_query,
    w_key,
    w_value,
    w_out,
    gain_head,
    w_head,
    b_head,
    points,
    pair_pose,
    new_points,
    new_pose,
    loss,
    feat,
    we,
    wq,
    wk,
    wv,
    wo,
    memory,
    keys,
    values,
    embedded,
    query_norm,
    query_diag,
    attended,
    pred,
    all_points,
    outgoing,
    incoming,
    load_sem,
    send_sem,
    recv_sem,
    pts_send,
    pts_recv,
    out_send,
    out_recv,
):
    own = lax.axis_index("img")
    core = own % 2
    y = (own // 2) % 2
    z = own // 4

    barrier = pltpu.get_barrier_semaphore()
    for k in range(1, NDEV):
        pl.semaphore_signal(
            barrier,
            inc=1,
            device_id={"img": (own + k) % NDEV},
            device_id_type=pl.DeviceIdType.MESH,
        )

    loads = []
    for slot, (src, dst) in enumerate(
        [(features, feat), (w_embed, we), (w_query, wq), (w_key, wk), (w_value, wv), (w_out, wo)]
    ):
        copy = pltpu.make_async_copy(src, dst, load_sem.at[slot])
        copy.start()
        loads.append(copy)

    def rank_of(zz, yy, cc):
        return (zz * 2 + yy) * 2 + cc

    targets = {
        UP: own + 4,
        DOWN: own - 4,
        ACROSS: rank_of(z, 1 - y, core),
        SIB: rank_of(z, y, 1 - core),
    }

    def move(piece, way):
        return pltpu.make_async_remote_copy(
            src_ref=memory.at[piece],
            dst_ref=memory.at[piece],
            send_sem=send_sem.at[piece * 4 + way],
            recv_sem=recv_sem.at[piece],
            device_id={"img": targets[way]},
            device_id_type=pl.DeviceIdType.MESH,
        )

    def arrive(piece):
        move(piece, SIB).wait_recv()

    side = z // 2
    near = z * (1 - side) + (3 - z) * side

    def origin_z(j):
        first = (4 - j) // 3 - (3 - j) // 3
        f = (j - near * first) * (1 - side) + (3 - j + near * first) * side
        zero = (3 - j) // 3
        return zero * z + (1 - zero) * f

    def same(a, b):
        return 1 // (1 + (a - b) * (a - b))

    def ends(zz):
        return (zz - 1) * (zz - 2) // 2

    end = ends(z)

    def pieces(tick, cc):
        k, ch = (tick + 1) // 2, (tick - 1) % 2
        two, three, five, seven = same(tick, 2), same(tick, 3), same(tick, 5), same(tick, 7)
        yj = end * ((tick - 1) // 2) + (1 - end) * (tick // 2 - two)
        ych = end * ((tick - 1) % 2) + (1 - end) * (two + five)
        bz = origin_z(3 - 2 * three)
        below = (rank_of(z - k, y, cc) * CHUNKS + ch, z - k >= 0)
        above = (rank_of(z + k, y, cc) * CHUNKS + ch, z + k <= 3)
        across = (rank_of(origin_z(yj), 1 - y, cc) * CHUNKS + ych, tick <= 6 + end)
        turned = (
            rank_of(bz, 1 - y, cc) * CHUNKS + 1,
            (1 - end) * (three + five) + end * seven == 1,
        )
        turn = same(yj, 0) * ych * end
        return below, above, across, turned, (k, ch, turn, bz)

    def forward(tick, act, before=None):
        below, above, across, turned, (k, ch, turn, bz) = pieces(tick, core)

        @pl.when(below[1])
        def _():
            if before is not None:
                before(below[0])

            @pl.when(z < 3)
            def _():
                act(below[0], UP)

            @pl.when(ch * ends(z - k) == 0)
            def _():
                act(below[0], ACROSS)

            act(below[0], SIB)

        @pl.when(above[1])
        def _():
            if before is not None:
                before(above[0])

            @pl.when(z > 0)
            def _():
                act(above[0], DOWN)

            @pl.when(ch * ends(z + k) == 0)
            def _():
                act(above[0], ACROSS)

            act(above[0], SIB)

        @pl.when(across[1])
        def _():
            if before is not None:
                before(across[0])

            @pl.when((turn == 1) & (z == 0))
            def _():
                act(across[0], UP)

            @pl.when((turn == 1) & (z == 3))
            def _():
                act(across[0], DOWN)

            act(across[0], SIB)

        @pl.when(turned[1])
        def _():
            if before is not None:
                before(turned[0])

            @pl.when((bz < z) & (z < 3))
            def _():
                act(turned[0], UP)

            @pl.when((bz > z) & (z > 0))
            def _():
                act(turned[0], DOWN)

            act(turned[0], SIB)

    def points_copy(peer, slot):
        return pltpu.make_async_remote_copy(
            src_ref=all_points.at[own],
            dst_ref=all_points.at[own],
            send_sem=pts_send.at[slot],
            recv_sem=pts_recv.at[own],
            device_id={"img": peer},
            device_id_type=pl.DeviceIdType.MESH,
        )

    def points_arrive(peer, slot):
        pltpu.make_async_remote_copy(
            src_ref=all_points.at[peer],
            dst_ref=all_points.at[peer],
            send_sem=pts_send.at[slot],
            recv_sem=pts_recv.at[peer],
            device_id={"img": peer},
            device_id_type=pl.DeviceIdType.MESH,
        ).wait_recv()

    all_points[own] = jnp.concatenate(
        [points[0], points[1], points[2], points[2]], axis=1
    )

    loads[0].wait()
    loads[1].wait()
    for ch in range(CHUNKS):
        rows = pl.ds(ch * CROWS, CROWS)
        emb = (dot(feat[rows, :], we[...]) + b_embed[...].reshape(1, D)).astype(BF16)
        embedded[rows, :] = emb
        emb_f = emb.astype(F32)
        center = emb_f - jnp.mean(emb_f, axis=-1, keepdims=True)
        unit = center * lax.rsqrt(jnp.mean(center * center, axis=-1, keepdims=True) + 1e-06)
        memory[own * CHUNKS + ch] = (unit * gain_memory[...].reshape(1, D)).astype(BF16)
        query_norm[rows, :] = (unit * gain_query[...].reshape(1, D)).astype(BF16)
        if ch == 0:
            pl.semaphore_wait(barrier, NDEV - 1)
            for k in range(1, NDEV):
                points_copy((own + k) % NDEV, k).start()
        piece = own * CHUNKS + ch

        move(piece, ACROSS).start()

        @pl.when(z < 3)
        def _():
            move(piece, UP).start()

        @pl.when(z > 0)
        def _():
            move(piece, DOWN).start()

        move(piece, SIB).start()

    loads[2].wait()
    group = lax.broadcasted_iota(jnp.int32, (256, 256), 0) // 64
    same_head = group == lax.broadcasted_iota(jnp.int32, (256, 256), 1) // 64

    def make_queries(i, carry):
        rows = pl.ds(pl.multiple_of(i * TOK, TOK), TOK)
        q = dot(query_norm[rows, :], wq[...]).astype(BF16).astype(F32) * 0.125
        for g in range(3):
            part = q[:, g * 256 : (g + 1) * 256]
            stacked = jnp.concatenate([part] * 4, axis=0)
            query_diag[i * 3 + g] = jnp.where(same_head, stacked, 0.0).astype(BF16)
        return carry

    lax.fori_loop(0, IMGS, make_queries, 0)

    loads[3].wait()
    loads[4].wait()
    loads[5].wait()

    def project(piece):
        rows = memory[piece]
        at = pl.ds(piece * CIMG, CIMG)
        keys[at] = dot(rows, wk[...]).astype(BF16).reshape(CIMG, TOK, D)
        values[at] = dot(rows, wv[...]).astype(BF16).reshape(CIMG, TOK, D)

    def project_all(tick, cc, before=None):
        for piece, valid in pieces(tick, cc)[:4]:

            @pl.when(valid)
            def _():
                if before is not None:
                    before(piece)
                project(piece)

    def own_sibling(ch, carry):
        piece = rank_of(z, y, 1 - core) * CHUNKS + ch
        arrive(piece)
        project(piece)
        return carry

    def exchange(tick, carry):
        @pl.when(tick <= 7)
        def _():
            forward(tick, lambda piece, way: move(piece, way).start(), arrive)

        @pl.when(tick >= 2)
        def _():
            project_all(tick - 1, 1 - core, arrive)

        @pl.when(tick <= 7)
        def _():
            project_all(tick, core)

        return carry

    lax.fori_loop(0, CHUNKS, own_sibling, 0)
    lax.fori_loop(1, 9, exchange, 0)

    for k in range(1, NDEV):
        points_arrive((own + k) % NDEV, k)
        points_copy((own + k) % NDEV, k).wait_send()

    lane = lax.broadcasted_iota(jnp.int32, (TOK, 128), 1)

    def image(i, carry):
        ids = [partners[p, own * IMGS + i] for p in range(PER)]
        key_rows = jnp.concatenate([keys[ids[p]] for p in range(PER)], axis=0)
        for g in range(3):
            scores = dot(
                key_rows[:, g * 256 : (g + 1) * 256], query_diag[i * 3 + g], ((1,), (1,))
            ).reshape(PER, TOK, 256)
            expo = jnp.exp(scores - jnp.max(scores, axis=1, keepdims=True))
            weights = (expo * (1.0 / jnp.sum(expo, axis=1, keepdims=True))).astype(BF16)
            for p in range(PER):
                for half in range(2):
                    lo = g * 256 + half * 128
                    both = dot(
                        weights[p, :, half * 128 : half * 128 + 128],
                        values[ids[p], :, lo : lo + 128],
                        ((0,), (0,)),
                    )
                    attended[p * TOK : (p + 1) * TOK, lo : lo + 128] = jnp.where(
                        lane < 64, both[:64], both[64:]
                    ).astype(BF16)
        projected = dot(attended[...], wo[...])
        emb_f = embedded[pl.ds(pl.multiple_of(i * TOK, TOK), TOK), :].astype(F32)
        decoded = projected.reshape(PER, TOK, D) + emb_f[None]
        head_in = norm_rows(decoded, gain_head[...].reshape(1, 1, D)).astype(BF16)
        out = dot(w_head[...], head_in.reshape(PER * TOK, D), ((1,), (1,)))
        for p in range(PER):
            pred[p * IMGS + i, 0:7, :] = out[:, p * TOK : (p + 1) * TOK]
        return carry

    lax.fori_loop(0, IMGS, image, 0)

    x = [pred[:, c, :] + b_head[c] for c in range(7)]
    conf = 1.0 + jnp.exp(x[6])
    view = lax.broadcasted_iota(jnp.int32, (VIEWS, 1), 0)
    ids = jnp.zeros((VIEWS, 1), jnp.int32)
    for v in range(VIEWS):
        ids = jnp.where(view == v, partners[v // IMGS, own * IMGS + v % IMGS], ids)
    hot = (ids == lax.broadcasted_iota(jnp.int32, (VIEWS, ALL), 1)).astype(F32)
    row = lax.broadcasted_iota(jnp.int32, (VIEWS, VIEWS), 0)
    col = lax.broadcasted_iota(jnp.int32, (VIEWS, VIEWS), 1)
    perm = ((row % IMGS) * PER + row // IMGS == col).astype(F32)
    pose = dot(perm, pair_pose[...], ((1,), (1,)), HI)
    partner_pts = dot(hot, all_points[...].reshape(ALL, 256), precision=HI)
    res_q, res_p = [], []
    for a in range(3):
        m = [pose[:, 3 * a + b : 3 * a + b + 1] for b in range(3)]
        off = pose[:, 9 + a : 10 + a]
        world_q = m[0] * x[0] + m[1] * x[1] + m[2] * x[2] + off
        world_p = m[0] * x[3] + m[1] * x[4] + m[2] * x[5] + off
        chi = jnp.concatenate([points[a]] * PER, axis=0)
        res_q.append(chi - world_q)
        res_p.append(partner_pts[:, a * TOK : (a + 1) * TOK] - world_p)
    cq = [conf * r for r in res_q]
    grad_rows = [
        jnp.sum(cq[a] * x[b], axis=1, keepdims=True) for a in range(3) for b in range(3)
    ] + [jnp.sum(cq[a], axis=1, keepdims=True) for a in range(3)]
    conf_row = jnp.sum(conf, axis=1, keepdims=True)
    step = jnp.concatenate(grad_rows, axis=1) * (2.0 / (4.0 * conf_row))
    new_pose[...] = pair_pose[...] + dot(step, perm, ((0,), (0,)), HI)
    err = jnp.sum(
        conf
        * (
            res_q[0] * res_q[0]
            + res_q[1] * res_q[1]
            + res_q[2] * res_q[2]
            + res_p[0] * res_p[0]
            + res_p[1] * res_p[1]
            + res_p[2] * res_p[2]
        )
    )
    conf_sum = 2.0 * jnp.sum(conf_row)
    payload = jnp.concatenate([conf * res_p[0], conf * res_p[1], conf * res_p[2], conf], axis=1)
    sums = dot(hot, payload, ((0,), (0,)), HI)
    outgoing[:, :, 0:256] = sums.reshape(NDEV, IMGS, 256)
    tail_lane = lax.broadcasted_iota(jnp.int32, (NDEV, IMGS, 128), 2)
    outgoing[:, :, 256:384] = jnp.where(tail_lane < 64, err, conf_sum)

    def out_copy(peer, slot):
        return pltpu.make_async_remote_copy(
            src_ref=outgoing.at[peer],
            dst_ref=incoming.at[own],
            send_sem=out_send.at[slot],
            recv_sem=out_recv.at[own],
            device_id={"img": peer},
            device_id_type=pl.DeviceIdType.MESH,
        )

    for k in range(1, NDEV):
        out_copy((own + k) % NDEV, k).start()
    incoming[own] = outgoing[own]

    def fold(values):
        total = values[0:IMGS]
        for p in range(1, PER):
            total = total + values[p * IMGS : (p + 1) * IMGS]
        return total

    total_q = fold(conf)
    grad_q = [fold(c) for c in cq]

    def drain(tick, carry):
        forward(tick, lambda piece, way: move(piece, way).wait_send())
        return carry

    lax.fori_loop(1, 8, drain, 0)
    for ch in range(CHUNKS):
        piece = own * CHUNKS + ch
        move(piece, ACROSS).wait_send()
        move(piece, SIB).wait_send()

        @pl.when(z < 3)
        def _():
            move(piece, UP).wait_send()

        @pl.when(z > 0)
        def _():
            move(piece, DOWN).wait_send()

    for k in range(1, NDEV):
        peer = (own + k) % NDEV
        pltpu.make_async_remote_copy(
            src_ref=outgoing.at[peer],
            dst_ref=incoming.at[peer],
            send_sem=out_send.at[k],
            recv_sem=out_recv.at[peer],
            device_id={"img": peer},
            device_id_type=pl.DeviceIdType.MESH,
        ).wait_recv()
        out_copy(peer, k).wait_send()
    received = jnp.sum(incoming[...], axis=0)
    total = total_q + received[:, 192:256]
    for a in range(3):
        grad = grad_q[a] + received[:, a * TOK : (a + 1) * TOK]
        new_points[a] = points[a] - 0.5 * grad / total
    loss[...] = received[0:1, 256:257] / received[0:1, 320:321]


def fused(*args):
    (
        features,
        partners,
        w_embed,
        b_embed,
        gain_query,
        gain_memory,
        w_query,
        w_key,
        w_value,
        w_out,
        gain_head,
        w_head,
        b_head,
        points,
        pair_pose,
    ) = args
    hbm = pl.BlockSpec(memory_space=pl.ANY)
    vmem = pl.BlockSpec(memory_space=pltpu.VMEM)
    smem = pl.BlockSpec(memory_space=pltpu.SMEM)
    rows = IMGS * TOK
    new_points, new_pose, loss = pl.pallas_call(
        kernel,
        out_shape=(
            jax.ShapeDtypeStruct((3, IMGS, TOK), F32),
            jax.ShapeDtypeStruct((12, VIEWS), F32),
            jax.ShapeDtypeStruct((1, 1), F32),
        ),
        in_specs=[
            hbm,
            smem,
            hbm,
            vmem,
            vmem,
            vmem,
            hbm,
            hbm,
            hbm,
            hbm,
            vmem,
            vmem,
            smem,
            vmem,
            vmem,
        ],
        out_specs=(vmem, vmem, vmem),
        scratch_shapes=[
            pltpu.VMEM((rows, E), BF16),
            pltpu.VMEM((E, D), BF16),
            pltpu.VMEM((D, D), BF16),
            pltpu.VMEM((D, D), BF16),
            pltpu.VMEM((D, D), BF16),
            pltpu.VMEM((D, D), BF16),
            pltpu.VMEM((NDEV * CHUNKS, CROWS, D), BF16),
            pltpu.VMEM((ALL, TOK, D), BF16),
            pltpu.VMEM((ALL, TOK, D), BF16),
            pltpu.VMEM((rows, D), BF16),
            pltpu.VMEM((rows, D), BF16),
            pltpu.VMEM((IMGS * 3, 256, 256), BF16),
            pltpu.VMEM((PER * TOK, D), BF16),
            pltpu.VMEM((VIEWS, 8, TOK), F32),
            pltpu.VMEM((NDEV, IMGS, 256), F32),
            pltpu.VMEM((NDEV, IMGS, 384), F32),
            pltpu.VMEM((NDEV, IMGS, 384), F32),
            pltpu.SemaphoreType.DMA((6,)),
            pltpu.SemaphoreType.DMA((NDEV * CHUNKS * 4,)),
            pltpu.SemaphoreType.DMA((NDEV * CHUNKS,)),
            pltpu.SemaphoreType.DMA((NDEV,)),
            pltpu.SemaphoreType.DMA((NDEV,)),
            pltpu.SemaphoreType.DMA((NDEV,)),
            pltpu.SemaphoreType.DMA((NDEV,)),
        ],
        compiler_params=pltpu.CompilerParams(
            collective_id=0, has_side_effects=True, vmem_limit_bytes=62 * 1024 * 1024
        ),
    )(
        features.reshape(rows, E),
        partners.T,
        w_embed,
        b_embed,
        gain_query,
        gain_memory,
        w_query,
        w_key,
        w_value,
        w_out,
        gain_head,
        w_head,
        b_head,
        points.transpose(1, 0, 2),
        pair_pose,
    )
    return new_points.transpose(1, 0, 2), new_pose, loss.reshape(1)


def layer_norm(values, gain):
    center = values - jnp.mean(values, axis=-1, keepdims=True)
    spread = jnp.mean(center * center, axis=-1, keepdims=True)
    return center * lax.rsqrt(spread + 1e-06) * gain


def per_device(
    features,
    partners,
    w_embed,
    b_embed,
    gain_query,
    gain_memory,
    w_query,
    w_key,
    w_value,
    w_out,
    gain_head,
    w_head,
    b_head,
    points,
    pair_pose,
):
    maximum_value = lax.Precision.HIGHEST
    count = lax.axis_size("img")
    own_index = lax.axis_index("img")
    img_dev, tokens_img, enc_width = features.shape
    width = w_query.shape[0]
    per_img = partners.shape[1]
    views = img_dev * per_img
    heads = HEADS
    head_size = width // heads
    capacity = max(2, (views + count - 2) // (count - 1))
    slots = count * capacity
    embedded = (
        jnp.dot(features.reshape(-1, enc_width), w_embed, preferred_element_type=jnp.float32)
        + b_embed
    ).astype(jnp.bfloat16)
    embed_f = embedded.astype(jnp.float32)
    query_norm = layer_norm(embed_f, gain_query).astype(jnp.bfloat16)
    memory_norm = layer_norm(embed_f, gain_memory).astype(jnp.bfloat16)
    queries = (
        jnp.dot(query_norm, w_query, preferred_element_type=jnp.float32)
        .astype(jnp.bfloat16)
        .reshape(img_dev, tokens_img, heads, head_size)
    )
    owners = (partners // img_dev).reshape(count, views)
    local_idx = (partners % img_dev).reshape(count, views)
    view_range = jnp.arange(views)
    earlier = view_range[:, None] > view_range[None, :]
    same_owner = owners[:, :, None] == owners[:, None, :]
    rank = jnp.sum(jnp.logical_and(same_owner, earlier[None]), axis=2)
    mine = owners == own_index
    select = jnp.logical_and(
        mine[:, :, None], rank[:, :, None] == jnp.arange(capacity)[None, None, :]
    ).astype(jnp.float32)
    local_hot = (local_idx[:, :, None] == jnp.arange(img_dev)[None, None, :]).astype(jnp.float32)
    pick = jnp.einsum("svc,svl->scl", select, local_hot, precision=maximum_value)
    pick_flat = pick.reshape(slots, img_dev).astype(jnp.bfloat16)
    my_owner = lax.dynamic_index_in_dim(owners, own_index, 0, keepdims=False)
    my_rank = lax.dynamic_index_in_dim(rank, own_index, 0, keepdims=False)
    slot_of_view = my_owner * capacity + my_rank
    placed = jnp.dot(
        pick_flat,
        memory_norm.reshape(img_dev, tokens_img * width),
        preferred_element_type=jnp.float32,
    )
    arrived = lax.all_to_all(
        placed.astype(jnp.bfloat16).reshape(count, capacity, tokens_img, width),
        "img",
        split_axis=0,
        concat_axis=0,
        tiled=True,
    )
    memory_views = jnp.take(
        arrived.reshape(slots, tokens_img, width), slot_of_view, axis=0
    ).reshape(views * tokens_img, width)
    key_views = jnp.dot(memory_views, w_key, preferred_element_type=jnp.float32).astype(
        jnp.bfloat16
    )
    value_views = jnp.dot(memory_views, w_value, preferred_element_type=jnp.float32).astype(
        jnp.bfloat16
    )
    key_views = key_views.reshape(img_dev, per_img, tokens_img, heads, head_size)
    value_views = value_views.reshape(img_dev, per_img, tokens_img, heads, head_size)
    scale = 1.0 / head_size**0.5
    scores = (
        jnp.einsum("ithd,ipshd->iphts", queries, key_views, preferred_element_type=jnp.float32)
        * scale
    )
    top = jnp.max(scores, axis=-1, keepdims=True)
    expo = jnp.exp(scores - top)
    weights = (expo / jnp.sum(expo, axis=-1, keepdims=True)).astype(jnp.bfloat16)
    attended = jnp.einsum(
        "iphts,ipshd->ipthd", weights, value_views, preferred_element_type=jnp.float32
    ).astype(jnp.bfloat16)
    projected = jnp.dot(
        attended.reshape(views * tokens_img, width), w_out, preferred_element_type=jnp.float32
    )
    decoded = embed_f.reshape(img_dev, 1, tokens_img, width) + projected.reshape(
        img_dev, per_img, tokens_img, width
    )
    head_in = layer_norm(decoded, gain_head).astype(jnp.bfloat16)
    pred = (
        jnp.einsum("iptd,cd->ipct", head_in, w_head, preferred_element_type=jnp.float32)
        + b_head[None, None, :, None]
    )
    pred = pred.reshape(views, 7, tokens_img)
    second_view_point = pred[:, 0:3]
    first_view_point = pred[:, 3:6]
    certainty_level = 1.0 + jnp.exp(pred[:, 6])
    pose_rows = pair_pose.T
    linear_transform = pose_rows[:, 0:9].reshape(views, 3, 3)
    translation_vector = pose_rows[:, 9:12]
    second_world_point = (
        jnp.einsum("xdp,xpk->xdk", linear_transform, second_view_point, precision=maximum_value)
        + translation_vector[:, :, None]
    )
    first_world_point = (
        jnp.einsum("xdp,xpk->xdk", linear_transform, first_view_point, precision=maximum_value)
        + translation_vector[:, :, None]
    )
    chi_views = jnp.broadcast_to(points[:, None], (img_dev, per_img, 3, tokens_img)).reshape(
        views, 3, tokens_img
    )
    second_residual = chi_views - second_world_point
    weighted_q = (certainty_level[:, None] * second_residual).reshape(
        img_dev, per_img, 3, tokens_img
    )
    grad_q = jnp.sum(weighted_q, axis=1)
    total_q = jnp.sum(certainty_level.reshape(img_dev, per_img, tokens_img), axis=1)
    gradient_transform = -2.0 * jnp.einsum(
        "zo,zpo,zso->zps",
        certainty_level,
        second_residual,
        second_view_point,
        precision=maximum_value,
    )
    grad_off = -2.0 * jnp.sum(certainty_level[:, None] * second_residual, axis=2)
    denom = 4.0 * jnp.sum(certainty_level, axis=1)
    grads = jnp.concatenate([gradient_transform.reshape(views, 9), grad_off], axis=1)
    new_pose = (pose_rows - grads / denom[:, None]).T
    err_q = jnp.sum(certainty_level * jnp.sum(second_residual * second_residual, axis=1))
    payload = jnp.concatenate([first_world_point, certainty_level[:, None]], axis=1)
    slot_hot = (slot_of_view[:, None] == jnp.arange(slots)[None, :]).astype(jnp.float32)
    outgoing = jnp.einsum("vk,vct->kct", slot_hot, payload, precision=maximum_value).reshape(
        count, capacity, 4, tokens_img
    )
    returned = lax.all_to_all(
        outgoing.astype(jnp.bfloat16), "img", split_axis=0, concat_axis=0, tiled=True
    ).astype(outgoing.dtype)
    ret_world = returned[:, :, 0:3]
    ret_conf = returned[:, :, 3]
    chi_slot = jnp.einsum("scl,lat->scat", pick, points, precision=maximum_value)
    res_p = chi_slot - ret_world
    grad_p = jnp.einsum(
        "scl,scat->lat", pick, ret_conf[:, :, None] * res_p, precision=maximum_value
    )
    total_p = jnp.einsum("scl,sct->lt", pick, ret_conf, precision=maximum_value)
    err_p = jnp.sum(ret_conf * jnp.sum(res_p * res_p, axis=2))
    new_points = points - 0.5 * (grad_q + grad_p) / (total_q + total_p)[:, None, :]
    err_sum, weight_sum = lax.psum((err_q + err_p, 2.0 * jnp.sum(certainty_level)), "img")
    loss = (err_sum / weight_sum).reshape(1)
    return (new_points, new_pose, loss)


def solution(mesh):
    return jax.shard_map(
        fused if mesh.shape["img"] == NDEV else per_device,
        mesh=mesh,
        in_specs=(
            P(("groups", "img"), None, None),
            P("groups", None),
            P(),
            P(),
            P(),
            P(),
            P(),
            P(),
            P(),
            P(),
            P(),
            P(),
            P(),
            P(("groups", "img"), None, None),
            P(None, ("groups", "img")),
        ),
        out_specs=(P(("groups", "img"), None, None), P(None, ("groups", "img")), P("groups")),
        check_vma=False,
    )
```

```python
import functools

import jax
import jax.numpy as jnp
from jax import lax
from jax.experimental import pallas as pl
from jax.experimental.pallas import tpu as pltpu
from jax.sharding import PartitionSpec as P

HEADS = 12
IMGS = 8
PER = 6
TOK = 64
VIEWS = IMGS * PER
E = 1024
D = 768
NDEV = 16
ALL = NDEV * IMGS
CHUNKS = 2
CROWS = IMGS * TOK // CHUNKS
CIMG = IMGS // CHUNKS
UP, DOWN, ACROSS, SIB = 0, 1, 2, 3
F32, BF16 = jnp.float32, jnp.bfloat16
HI = lax.Precision.HIGHEST


def norm_rows(values, gain):
    center = values - jnp.mean(values, axis=-1, keepdims=True)
    spread = jnp.mean(center * center, axis=-1, keepdims=True)
    return center * lax.rsqrt(spread + 1e-06) * gain


def dot(a, b, dims=((1,), (0,)), precision=None):
    return lax.dot_general(a, b, (dims, ((), ())), precision=precision, preferred_element_type=F32)


def kernel(
    features,
    partners,
    w_embed,
    b_embed,
    gain_query,
    gain_memory,
    w_query,
    w_key,
    w_value,
    w_out,
    gain_head,
    w_head,
    b_head,
    points,
    pair_pose,
    new_points,
    new_pose,
    loss,
    feat,
    we,
    wq,
    wk,
    wv,
    wo,
    memory,
    keys,
    values,
    embedded,
    query_norm,
    query_diag,
    attended,
    pred,
    all_points,
    outgoing,
    incoming,
    load_sem,
    send_sem,
    recv_sem,
    pts_send,
    pts_recv,
    out_send,
    out_recv,
):
    own = lax.axis_index("img")
    core = own % 2
    y = (own // 2) % 2
    z = own // 4

    barrier = pltpu.get_barrier_semaphore()
    for k in range(1, NDEV):
        pl.semaphore_signal(
            barrier,
            inc=1,
            device_id={"img": (own + k) % NDEV},
            device_id_type=pl.DeviceIdType.MESH,
        )

    loads = []
    for slot, (src, dst) in enumerate(
        [(features, feat), (w_embed, we), (w_query, wq), (w_key, wk), (w_value, wv), (w_out, wo)]
    ):
        copy = pltpu.make_async_copy(src, dst, load_sem.at[slot])
        copy.start()
        loads.append(copy)

    def rank_of(zz, yy, cc):
        return (zz * 2 + yy) * 2 + cc

    targets = {
        UP: own + 4,
        DOWN: own - 4,
        ACROSS: rank_of(z, 1 - y, core),
        SIB: rank_of(z, y, 1 - core),
    }

    def move(piece, way):
        return pltpu.make_async_remote_copy(
            src_ref=memory.at[piece],
            dst_ref=memory.at[piece],
            send_sem=send_sem.at[piece * 4 + way],
            recv_sem=recv_sem.at[piece],
            device_id={"img": targets[way]},
            device_id_type=pl.DeviceIdType.MESH,
        )

    def arrive(piece):
        move(piece, SIB).wait_recv()

    side = z // 2
    near = z * (1 - side) + (3 - z) * side

    def origin_z(j):
        first = (4 - j) // 3 - (3 - j) // 3
        f = (j - near * first) * (1 - side) + (3 - j + near * first) * side
        zero = (3 - j) // 3
        return zero * z + (1 - zero) * f

    def same(a, b):
        return 1 // (1 + (a - b) * (a - b))

    def ends(zz):
        return (zz - 1) * (zz - 2) // 2

    end = ends(z)

    def pieces(tick, cc):
        k, ch = (tick + 1) // 2, (tick - 1) % 2
        two, three, five, seven = same(tick, 2), same(tick, 3), same(tick, 5), same(tick, 7)
        yj = end * ((tick - 1) // 2) + (1 - end) * (tick // 2 - two)
        ych = end * ((tick - 1) % 2) + (1 - end) * (two + five)
        bz = origin_z(3 - 2 * three)
        below = (rank_of(z - k, y, cc) * CHUNKS + ch, z - k >= 0)
        above = (rank_of(z + k, y, cc) * CHUNKS + ch, z + k <= 3)
        across = (rank_of(origin_z(yj), 1 - y, cc) * CHUNKS + ych, tick <= 6 + end)
        turned = (
            rank_of(bz, 1 - y, cc) * CHUNKS + 1,
            (1 - end) * (three + five) + end * seven == 1,
        )
        turn = same(yj, 0) * ych * end
        return below, above, across, turned, (k, ch, turn, bz)

    def forward(tick, act, before=None):
        below, above, across, turned, (k, ch, turn, bz) = pieces(tick, core)

        @pl.when(below[1])
        def _():
            if before is not None:
                before(below[0])

            @pl.when(z < 3)
            def _():
                act(below[0], UP)

            @pl.when(ch * ends(z - k) == 0)
            def _():
                act(below[0], ACROSS)

            act(below[0], SIB)

        @pl.when(above[1])
        def _():
            if before is not None:
                before(above[0])

            @pl.when(z > 0)
            def _():
                act(above[0], DOWN)

            @pl.when(ch * ends(z + k) == 0)
            def _():
                act(above[0], ACROSS)

            act(above[0], SIB)

        @pl.when(across[1])
        def _():
            if before is not None:
                before(across[0])

            @pl.when((turn == 1) & (z == 0))
            def _():
                act(across[0], UP)

            @pl.when((turn == 1) & (z == 3))
            def _():
                act(across[0], DOWN)

            act(across[0], SIB)

        @pl.when(turned[1])
        def _():
            if before is not None:
                before(turned[0])

            @pl.when((bz < z) & (z < 3))
            def _():
                act(turned[0], UP)

            @pl.when((bz > z) & (z > 0))
            def _():
                act(turned[0], DOWN)

            act(turned[0], SIB)

    def points_copy(peer, slot):
        return pltpu.make_async_remote_copy(
            src_ref=all_points.at[own],
            dst_ref=all_points.at[own],
            send_sem=pts_send.at[slot],
            recv_sem=pts_recv.at[own],
            device_id={"img": peer},
            device_id_type=pl.DeviceIdType.MESH,
        )

    def points_arrive(peer, slot):
        pltpu.make_async_remote_copy(
            src_ref=all_points.at[peer],
            dst_ref=all_points.at[peer],
            send_sem=pts_send.at[slot],
            recv_sem=pts_recv.at[peer],
            device_id={"img": peer},
            device_id_type=pl.DeviceIdType.MESH,
        ).wait_recv()

    all_points[own] = jnp.concatenate(
        [points[0], points[1], points[2], points[2]], axis=1
    )

    loads[0].wait()
    loads[1].wait()
    for ch in range(CHUNKS):
        rows = pl.ds(ch * CROWS, CROWS)
        emb = (dot(feat[rows, :], we[...]) + b_embed[...].reshape(1, D)).astype(BF16)
        embedded[rows, :] = emb
        emb_f = emb.astype(F32)
        center = emb_f - jnp.mean(emb_f, axis=-1, keepdims=True)
        unit = center * lax.rsqrt(jnp.mean(center * center, axis=-1, keepdims=True) + 1e-06)
        memory[own * CHUNKS + ch] = (unit * gain_memory[...].reshape(1, D)).astype(BF16)
        query_norm[rows, :] = (unit * gain_query[...].reshape(1, D)).astype(BF16)
        if ch == 0:
            pl.semaphore_wait(barrier, NDEV - 1)
        piece = own * CHUNKS + ch

        move(piece, ACROSS).start()

        @pl.when(z < 3)
        def _():
            move(piece, UP).start()

        @pl.when(z > 0)
        def _():
            move(piece, DOWN).start()

        move(piece, SIB).start()
        if ch == 0:
            for k in range(1, NDEV):
                points_copy((own + k) % NDEV, k).start()

    loads[2].wait()
    group = lax.broadcasted_iota(jnp.int32, (256, 256), 0) // 64
    same_head = group == lax.broadcasted_iota(jnp.int32, (256, 256), 1) // 64

    def make_queries(i, carry):
        rows = pl.ds(pl.multiple_of(i * TOK, TOK), TOK)
        q = dot(query_norm[rows, :], wq[...]).astype(BF16).astype(F32) * 0.125
        for g in range(3):
            part = q[:, g * 256 : (g + 1) * 256]
            stacked = jnp.concatenate([part] * 4, axis=0)
            query_diag[i * 3 + g] = jnp.where(same_head, stacked, 0.0).astype(BF16)
        return carry

    lax.fori_loop(0, IMGS, make_queries, 0)

    loads[3].wait()
    loads[4].wait()
    loads[5].wait()

    def project(piece):
        rows = memory[piece]
        at = pl.ds(piece * CIMG, CIMG)
        keys[at] = dot(rows, wk[...]).astype(BF16).reshape(CIMG, TOK, D)
        values[at] = dot(rows, wv[...]).astype(BF16).reshape(CIMG, TOK, D)

    def project_all(tick, cc, before=None):
        for piece, valid in pieces(tick, cc)[:4]:

            @pl.when(valid)
            def _():
                if before is not None:
                    before(piece)
                project(piece)

    def own_sibling(ch, carry):
        piece = rank_of(z, y, 1 - core) * CHUNKS + ch
        arrive(piece)
        project(piece)
        return carry

    def exchange(tick, carry):
        @pl.when(tick <= 7)
        def _():
            forward(tick, lambda piece, way: move(piece, way).start(), arrive)

        @pl.when(tick >= 2)
        def _():
            project_all(tick - 1, 1 - core, arrive)

        @pl.when(tick <= 7)
        def _():
            project_all(tick, core)

        return carry

    for k in range(1, NDEV):
        points_arrive((own + k) % NDEV, k)
        points_copy((own + k) % NDEV, k).wait_send()

    view = lax.broadcasted_iota(jnp.int32, (VIEWS, 1), 0)
    ids = jnp.zeros((VIEWS, 1), jnp.int32)
    for v in range(VIEWS):
        ids = jnp.where(view == v, partners[v // IMGS, own * IMGS + v % IMGS], ids)
    hot = (ids == lax.broadcasted_iota(jnp.int32, (VIEWS, ALL), 1)).astype(F32)
    row = lax.broadcasted_iota(jnp.int32, (VIEWS, VIEWS), 0)
    col = lax.broadcasted_iota(jnp.int32, (VIEWS, VIEWS), 1)
    perm = ((row % IMGS) * PER + row // IMGS == col).astype(F32)
    pose = dot(perm, pair_pose[...], ((1,), (1,)), HI)
    partner_pts = dot(hot, all_points[...].reshape(ALL, 256), precision=HI)

    lax.fori_loop(0, CHUNKS, own_sibling, 0)
    lax.fori_loop(1, 9, exchange, 0)

    lane = lax.broadcasted_iota(jnp.int32, (TOK, 128), 1)

    def image(i, carry):
        ids = [partners[p, own * IMGS + i] for p in range(PER)]
        key_rows = jnp.concatenate([keys[ids[p]] for p in range(PER)], axis=0)
        for g in range(3):
            scores = dot(
                key_rows[:, g * 256 : (g + 1) * 256], query_diag[i * 3 + g], ((1,), (1,))
            ).reshape(PER, TOK, 256)
            expo = jnp.exp(scores - jnp.max(scores, axis=1, keepdims=True))
            weights = (expo * (1.0 / jnp.sum(expo, axis=1, keepdims=True))).astype(BF16)
            for p in range(PER):
                for half in range(2):
                    lo = g * 256 + half * 128
                    both = dot(
                        weights[p, :, half * 128 : half * 128 + 128],
                        values[ids[p], :, lo : lo + 128],
                        ((0,), (0,)),
                    )
                    attended[p * TOK : (p + 1) * TOK, lo : lo + 128] = jnp.where(
                        lane < 64, both[:64], both[64:]
                    ).astype(BF16)
        projected = dot(attended[...], wo[...])
        emb_f = embedded[pl.ds(pl.multiple_of(i * TOK, TOK), TOK), :].astype(F32)
        decoded = projected.reshape(PER, TOK, D) + emb_f[None]
        head_in = norm_rows(decoded, gain_head[...].reshape(1, 1, D)).astype(BF16)
        out = dot(w_head[...], head_in.reshape(PER * TOK, D), ((1,), (1,)))
        for p in range(PER):
            pred[p * IMGS + i, 0:7, :] = out[:, p * TOK : (p + 1) * TOK]
        return carry

    lax.fori_loop(0, IMGS, image, 0)

    x = [pred[:, c, :] + b_head[c] for c in range(7)]
    conf = 1.0 + jnp.exp(x[6])
    res_q, res_p = [], []
    for a in range(3):
        m = [pose[:, 3 * a + b : 3 * a + b + 1] for b in range(3)]
        off = pose[:, 9 + a : 10 + a]
        world_q = m[0] * x[0] + m[1] * x[1] + m[2] * x[2] + off
        world_p = m[0] * x[3] + m[1] * x[4] + m[2] * x[5] + off
        chi = jnp.concatenate([points[a]] * PER, axis=0)
        res_q.append(chi - world_q)
        res_p.append(partner_pts[:, a * TOK : (a + 1) * TOK] - world_p)
    cq = [conf * r for r in res_q]
    grad_rows = [
        jnp.sum(cq[a] * x[b], axis=1, keepdims=True) for a in range(3) for b in range(3)
    ] + [jnp.sum(cq[a], axis=1, keepdims=True) for a in range(3)]
    conf_row = jnp.sum(conf, axis=1, keepdims=True)
    step = jnp.concatenate(grad_rows, axis=1) * (2.0 / (4.0 * conf_row))
    new_pose[...] = pair_pose[...] + dot(step, perm, ((0,), (0,)), HI)
    err = jnp.sum(
        conf
        * (
            res_q[0] * res_q[0]
            + res_q[1] * res_q[1]
            + res_q[2] * res_q[2]
            + res_p[0] * res_p[0]
            + res_p[1] * res_p[1]
            + res_p[2] * res_p[2]
        )
    )
    conf_sum = 2.0 * jnp.sum(conf_row)
    payload = jnp.concatenate([conf * res_p[0], conf * res_p[1], conf * res_p[2], conf], axis=1)
    sums = dot(hot, payload, ((0,), (0,)), HI)
    outgoing[:, :, 0:256] = sums.reshape(NDEV, IMGS, 256)
    tail_lane = lax.broadcasted_iota(jnp.int32, (NDEV, IMGS, 128), 2)
    outgoing[:, :, 256:384] = jnp.where(tail_lane < 64, err, conf_sum)

    def out_copy(peer, slot):
        return pltpu.make_async_remote_copy(
            src_ref=outgoing.at[peer],
            dst_ref=incoming.at[own],
            send_sem=out_send.at[slot],
            recv_sem=out_recv.at[own],
            device_id={"img": peer},
            device_id_type=pl.DeviceIdType.MESH,
        )

    for k in range(1, NDEV):
        out_copy((own + k) % NDEV, k).start()
    incoming[own] = outgoing[own]

    def fold(values):
        total = values[0:IMGS]
        for p in range(1, PER):
            total = total + values[p * IMGS : (p + 1) * IMGS]
        return total

    total_q = fold(conf)
    grad_q = [fold(c) for c in cq]

    def drain(tick, carry):
        forward(tick, lambda piece, way: move(piece, way).wait_send())
        return carry

    lax.fori_loop(1, 8, drain, 0)
    for ch in range(CHUNKS):
        piece = own * CHUNKS + ch
        move(piece, ACROSS).wait_send()
        move(piece, SIB).wait_send()

        @pl.when(z < 3)
        def _():
            move(piece, UP).wait_send()

        @pl.when(z > 0)
        def _():
            move(piece, DOWN).wait_send()

    for k in range(1, NDEV):
        peer = (own + k) % NDEV
        pltpu.make_async_remote_copy(
            src_ref=outgoing.at[peer],
            dst_ref=incoming.at[peer],
            send_sem=out_send.at[k],
            recv_sem=out_recv.at[peer],
            device_id={"img": peer},
            device_id_type=pl.DeviceIdType.MESH,
        ).wait_recv()
        out_copy(peer, k).wait_send()
    received = jnp.sum(incoming[...], axis=0)
    total = total_q + received[:, 192:256]
    for a in range(3):
        grad = grad_q[a] + received[:, a * TOK : (a + 1) * TOK]
        new_points[a] = points[a] - 0.5 * grad / total
    loss[...] = received[0:1, 256:257] / received[0:1, 320:321]


def fused(*args):
    (
        features,
        partners,
        w_embed,
        b_embed,
        gain_query,
        gain_memory,
        w_query,
        w_key,
        w_value,
        w_out,
        gain_head,
        w_head,
        b_head,
        points,
        pair_pose,
    ) = args
    hbm = pl.BlockSpec(memory_space=pl.ANY)
    vmem = pl.BlockSpec(memory_space=pltpu.VMEM)
    smem = pl.BlockSpec(memory_space=pltpu.SMEM)
    rows = IMGS * TOK
    new_points, new_pose, loss = pl.pallas_call(
        kernel,
        out_shape=(
            jax.ShapeDtypeStruct((3, IMGS, TOK), F32),
            jax.ShapeDtypeStruct((12, VIEWS), F32),
            jax.ShapeDtypeStruct((1, 1), F32),
        ),
        in_specs=[
            hbm,
            smem,
            hbm,
            vmem,
            vmem,
            vmem,
            hbm,
            hbm,
            hbm,
            hbm,
            vmem,
            vmem,
            smem,
            vmem,
            vmem,
        ],
        out_specs=(vmem, vmem, vmem),
        scratch_shapes=[
            pltpu.VMEM((rows, E), BF16),
            pltpu.VMEM((E, D), BF16),
            pltpu.VMEM((D, D), BF16),
            pltpu.VMEM((D, D), BF16),
            pltpu.VMEM((D, D), BF16),
            pltpu.VMEM((D, D), BF16),
            pltpu.VMEM((NDEV * CHUNKS, CROWS, D), BF16),
            pltpu.VMEM((ALL, TOK, D), BF16),
            pltpu.VMEM((ALL, TOK, D), BF16),
            pltpu.VMEM((rows, D), BF16),
            pltpu.VMEM((rows, D), BF16),
            pltpu.VMEM((IMGS * 3, 256, 256), BF16),
            pltpu.VMEM((PER * TOK, D), BF16),
            pltpu.VMEM((VIEWS, 8, TOK), F32),
            pltpu.VMEM((NDEV, IMGS, 256), F32),
            pltpu.VMEM((NDEV, IMGS, 384), F32),
            pltpu.VMEM((NDEV, IMGS, 384), F32),
            pltpu.SemaphoreType.DMA((6,)),
            pltpu.SemaphoreType.DMA((NDEV * CHUNKS * 4,)),
            pltpu.SemaphoreType.DMA((NDEV * CHUNKS,)),
            pltpu.SemaphoreType.DMA((NDEV,)),
            pltpu.SemaphoreType.DMA((NDEV,)),
            pltpu.SemaphoreType.DMA((NDEV,)),
            pltpu.SemaphoreType.DMA((NDEV,)),
        ],
        compiler_params=pltpu.CompilerParams(
            collective_id=0, has_side_effects=True, vmem_limit_bytes=62 * 1024 * 1024
        ),
    )(
        features.reshape(rows, E),
        partners.T,
        w_embed,
        b_embed,
        gain_query,
        gain_memory,
        w_query,
        w_key,
        w_value,
        w_out,
        gain_head,
        w_head,
        b_head,
        points.transpose(1, 0, 2),
        pair_pose,
    )
    return new_points.transpose(1, 0, 2), new_pose, loss.reshape(1)


def layer_norm(values, gain):
    center = values - jnp.mean(values, axis=-1, keepdims=True)
    spread = jnp.mean(center * center, axis=-1, keepdims=True)
    return center * lax.rsqrt(spread + 1e-06) * gain


def per_device(
    features,
    partners,
    w_embed,
    b_embed,
    gain_query,
    gain_memory,
    w_query,
    w_key,
    w_value,
    w_out,
    gain_head,
    w_head,
    b_head,
    points,
    pair_pose,
):
    maximum_value = lax.Precision.HIGHEST
    count = lax.axis_size("img")
    own_index = lax.axis_index("img")
    img_dev, tokens_img, enc_width = features.shape
    width = w_query.shape[0]
    per_img = partners.shape[1]
    views = img_dev * per_img
    heads = HEADS
    head_size = width // heads
    capacity = max(2, (views + count - 2) // (count - 1))
    slots = count * capacity
    embedded = (
        jnp.dot(features.reshape(-1, enc_width), w_embed, preferred_element_type=jnp.float32)
        + b_embed
    ).astype(jnp.bfloat16)
    embed_f = embedded.astype(jnp.float32)
    query_norm = layer_norm(embed_f, gain_query).astype(jnp.bfloat16)
    memory_norm = layer_norm(embed_f, gain_memory).astype(jnp.bfloat16)
    queries = (
        jnp.dot(query_norm, w_query, preferred_element_type=jnp.float32)
        .astype(jnp.bfloat16)
        .reshape(img_dev, tokens_img, heads, head_size)
    )
    owners = (partners // img_dev).reshape(count, views)
    local_idx = (partners % img_dev).reshape(count, views)
    view_range = jnp.arange(views)
    earlier = view_range[:, None] > view_range[None, :]
    same_owner = owners[:, :, None] == owners[:, None, :]
    rank = jnp.sum(jnp.logical_and(same_owner, earlier[None]), axis=2)
    mine = owners == own_index
    select = jnp.logical_and(
        mine[:, :, None], rank[:, :, None] == jnp.arange(capacity)[None, None, :]
    ).astype(jnp.float32)
    local_hot = (local_idx[:, :, None] == jnp.arange(img_dev)[None, None, :]).astype(jnp.float32)
    pick = jnp.einsum("svc,svl->scl", select, local_hot, precision=maximum_value)
    pick_flat = pick.reshape(slots, img_dev).astype(jnp.bfloat16)
    my_owner = lax.dynamic_index_in_dim(owners, own_index, 0, keepdims=False)
    my_rank = lax.dynamic_index_in_dim(rank, own_index, 0, keepdims=False)
    slot_of_view = my_owner * capacity + my_rank
    placed = jnp.dot(
        pick_flat,
        memory_norm.reshape(img_dev, tokens_img * width),
        preferred_element_type=jnp.float32,
    )
    arrived = lax.all_to_all(
        placed.astype(jnp.bfloat16).reshape(count, capacity, tokens_img, width),
        "img",
        split_axis=0,
        concat_axis=0,
        tiled=True,
    )
    memory_views = jnp.take(
        arrived.reshape(slots, tokens_img, width), slot_of_view, axis=0
    ).reshape(views * tokens_img, width)
    key_views = jnp.dot(memory_views, w_key, preferred_element_type=jnp.float32).astype(
        jnp.bfloat16
    )
    value_views = jnp.dot(memory_views, w_value, preferred_element_type=jnp.float32).astype(
        jnp.bfloat16
    )
    key_views = key_views.reshape(img_dev, per_img, tokens_img, heads, head_size)
    value_views = value_views.reshape(img_dev, per_img, tokens_img, heads, head_size)
    scale = 1.0 / head_size**0.5
    scores = (
        jnp.einsum("ithd,ipshd->iphts", queries, key_views, preferred_element_type=jnp.float32)
        * scale
    )
    top = jnp.max(scores, axis=-1, keepdims=True)
    expo = jnp.exp(scores - top)
    weights = (expo / jnp.sum(expo, axis=-1, keepdims=True)).astype(jnp.bfloat16)
    attended = jnp.einsum(
        "iphts,ipshd->ipthd", weights, value_views, preferred_element_type=jnp.float32
    ).astype(jnp.bfloat16)
    projected = jnp.dot(
        attended.reshape(views * tokens_img, width), w_out, preferred_element_type=jnp.float32
    )
    decoded = embed_f.reshape(img_dev, 1, tokens_img, width) + projected.reshape(
        img_dev, per_img, tokens_img, width
    )
    head_in = layer_norm(decoded, gain_head).astype(jnp.bfloat16)
    pred = (
        jnp.einsum("iptd,cd->ipct", head_in, w_head, preferred_element_type=jnp.float32)
        + b_head[None, None, :, None]
    )
    pred = pred.reshape(views, 7, tokens_img)
    second_view_point = pred[:, 0:3]
    first_view_point = pred[:, 3:6]
    certainty_level = 1.0 + jnp.exp(pred[:, 6])
    pose_rows = pair_pose.T
    linear_transform = pose_rows[:, 0:9].reshape(views, 3, 3)
    translation_vector = pose_rows[:, 9:12]
    second_world_point = (
        jnp.einsum("xdp,xpk->xdk", linear_transform, second_view_point, precision=maximum_value)
        + translation_vector[:, :, None]
    )
    first_world_point = (
        jnp.einsum("xdp,xpk->xdk", linear_transform, first_view_point, precision=maximum_value)
        + translation_vector[:, :, None]
    )
    chi_views = jnp.broadcast_to(points[:, None], (img_dev, per_img, 3, tokens_img)).reshape(
        views, 3, tokens_img
    )
    second_residual = chi_views - second_world_point
    weighted_q = (certainty_level[:, None] * second_residual).reshape(
        img_dev, per_img, 3, tokens_img
    )
    grad_q = jnp.sum(weighted_q, axis=1)
    total_q = jnp.sum(certainty_level.reshape(img_dev, per_img, tokens_img), axis=1)
    gradient_transform = -2.0 * jnp.einsum(
        "zo,zpo,zso->zps",
        certainty_level,
        second_residual,
        second_view_point,
        precision=maximum_value,
    )
    grad_off = -2.0 * jnp.sum(certainty_level[:, None] * second_residual, axis=2)
    denom = 4.0 * jnp.sum(certainty_level, axis=1)
    grads = jnp.concatenate([gradient_transform.reshape(views, 9), grad_off], axis=1)
    new_pose = (pose_rows - grads / denom[:, None]).T
    err_q = jnp.sum(certainty_level * jnp.sum(second_residual * second_residual, axis=1))
    payload = jnp.concatenate([first_world_point, certainty_level[:, None]], axis=1)
    slot_hot = (slot_of_view[:, None] == jnp.arange(slots)[None, :]).astype(jnp.float32)
    outgoing = jnp.einsum("vk,vct->kct", slot_hot, payload, precision=maximum_value).reshape(
        count, capacity, 4, tokens_img
    )
    returned = lax.all_to_all(
        outgoing.astype(jnp.bfloat16), "img", split_axis=0, concat_axis=0, tiled=True
    ).astype(outgoing.dtype)
    ret_world = returned[:, :, 0:3]
    ret_conf = returned[:, :, 3]
    chi_slot = jnp.einsum("scl,lat->scat", pick, points, precision=maximum_value)
    res_p = chi_slot - ret_world
    grad_p = jnp.einsum(
        "scl,scat->lat", pick, ret_conf[:, :, None] * res_p, precision=maximum_value
    )
    total_p = jnp.einsum("scl,sct->lt", pick, ret_conf, precision=maximum_value)
    err_p = jnp.sum(ret_conf * jnp.sum(res_p * res_p, axis=2))
    new_points = points - 0.5 * (grad_q + grad_p) / (total_q + total_p)[:, None, :]
    err_sum, weight_sum = lax.psum((err_q + err_p, 2.0 * jnp.sum(certainty_level)), "img")
    loss = (err_sum / weight_sum).reshape(1)
    return (new_points, new_pose, loss)


def solution(mesh):
    return jax.shard_map(
        fused if mesh.shape["img"] == NDEV else per_device,
        mesh=mesh,
        in_specs=(
            P(("groups", "img"), None, None),
            P("groups", None),
            P(),
            P(),
            P(),
            P(),
            P(),
            P(),
            P(),
            P(),
            P(),
            P(),
            P(),
            P(("groups", "img"), None, None),
            P(None, ("groups", "img")),
        ),
        out_specs=(P(("groups", "img"), None, None), P(None, ("groups", "img")), P("groups")),
        check_vma=False,
    )
```
